32 devices in a mesh: grp: 2 (over y), tm: 16 (over z, x, core).
Axes of the slice: x: 2, y: 2, z: 4, core: 2. Of those that a mesh axis runs over, the one named last changes fastest.
Arguments:
- state: float32 [256, 16, 8192], P(('grp', 'tm')), parts along dimension 0, may hold values from -6 to 6
- forcing: float32 [256, 16, 8192], P(('grp', 'tm')), parts along dimension 0, may hold values from -6 to 6
- noise_weight: float32 [256, 8192], P(('grp', 'tm')), parts along dimension 0, may hold values from 0.5 to 2
- prev_coupling: float32 [8192], replicated, may hold values from 0.3 to 1
- next_coupling: float32 [8192], replicated, may hold values from 0.3 to 1
- block_values: bfloat16 [64, 4, 128, 128], replicated, may hold values from -0.25 to 0.25
- block_pattern: int32 [64, 4], replicated, may hold values from 0 to 63, all different within a row
Outputs:
- gradient: float32 [256, 16, 8192], P(('grp', 'tm')), parts along dimension 0
- log_density: float32 [32], P('grp'), parts along dimension 0
The draws below stay inside these ranges and needn't reach their ends.
There are 2 independent parts, one for each index of `grp`. The reference program is written for one: setup_inputs(seed, part) draws one part's arguments, and reference() takes and returns one part's arrays. A program takes and returns all parts, laid end to end along the dimension named above; an argument that names none is the same for every part. Nothing has to cross between parts.
Inputs may be any that keep to these rules, and one draw needn't show every extreme that they name: `block_pattern`: the 4 entries of a row are distinct, and every block is named by some row.
All inputs are finite; a program needn't handle non-finite values.
Results may differ from the reference program's by a relative error of at most 0.0026.
Values sent between devices are 32-bit elements; how exact they have to be, the bound alone decides.
A program may use at most 128 MiB of HBM per device.

```python
import math
import jax
import jax.numpy as jnp
from jax import lax

BLOCK = 128
SAMPLES = 16
LINKS = 4
BLOCKS = 64
NODES = 8192
DAYS = 128


def draw_state(key, part):
    day_index = jnp.arange(DAYS, dtype=jnp.float32)
    scale = (0.5 + day_index / DAYS)[:, None, None]
    values = jax.random.normal(key, (DAYS, SAMPLES, NODES), jnp.float32) * scale
    return jnp.clip(values, -6.0, 6.0)


def steps_of(key, extent, pieces, least, largest):
    level = 1.0
    for dim, shards_of in pieces:
        draws = jax.random.uniform(jax.random.fold_in(jax.random.fold_in(key, 6), dim), (shards_of,), jnp.float32, least / len(pieces), largest / len(pieces))
        level = level * jnp.repeat(jnp.exp(draws), extent[dim] // shards_of).reshape((-1,) + (1,) * (len(extent) - 1 - dim))
    return level


def choose_distinct(key, rows, count, top, lift):
    ranking = jax.random.permutation(jax.random.fold_in(key, 1), count)
    favour = ranking
    for power in range(3):
        favour = favour * favour // count
    favour = favour * lift // count
    tickets = jax.random.randint(jax.random.fold_in(key, 2), (rows, count), 0, 4096) + favour
    fixed_rows = jax.random.permutation(jax.random.fold_in(key, 3), rows)[jnp.arange(count) % rows]
    tickets = jnp.where(jnp.arange(rows)[:, None] == fixed_rows[None, :], 1 << 14, tickets)
    merit = tickets * count + jnp.arange(count)
    return lax.top_k(merit.astype(jnp.int32), top)[1].astype(jnp.int32)


def scatter_about(stream_key, shape, scale, most, shards=(), kind=jnp.bfloat16):
    drawn = scale * jax.random.normal(stream_key, shape, jnp.float32)
    if shards:
        drawn = drawn * steps_of(stream_key, shape, shards, -0.22, 0.18)
    return jnp.clip(drawn, -most, most).astype(kind)


def setup_inputs(seed: int = 0, part: int = 0) -> dict:
    key_list = jax.random.split(jax.random.key(seed), 8)
    part_splits = jax.random.split(jax.random.fold_in(key_list[7], part), 8)
    state = draw_state(jax.random.fold_in(jax.random.fold_in(key_list[7], part), 71), part)
    forcing = scatter_about(part_splits[1], (DAYS, SAMPLES, NODES), 1.0, 6.0, ((0, 16),), jnp.float32)
    noise_weight = jnp.clip(jnp.exp(math.log(2.0) - 1.3862944 * jax.random.uniform(part_splits[2], (DAYS, NODES), jnp.float32) ** steps_of(part_splits[2], (DAYS, NODES), ((0, 16),), -0.2, 0.2)), 0.5, 2.0)
    prev_coupling = jnp.clip(jax.random.uniform(key_list[3], (NODES,), jnp.float32, 0.3, 1.0), 0.3, 1.0)
    next_coupling = jnp.clip(jax.random.uniform(key_list[4], (NODES,), jnp.float32, 0.3, 1.0), 0.3, 1.0)
    block_values = scatter_about(key_list[5], (BLOCKS, LINKS, BLOCK, BLOCK), (LINKS * BLOCK) ** -0.5, 0.25)
    block_pattern = choose_distinct(key_list[6], BLOCKS, BLOCKS, LINKS, 0)
    return {"state": state, "forcing": forcing, "noise_weight": noise_weight, "prev_coupling": prev_coupling, "next_coupling": next_coupling, "block_values": block_values, "block_pattern": block_pattern}


def spatial_day(day_rounded, block_values, block_pattern):
    blocks = day_rounded.reshape(SAMPLES, BLOCKS, BLOCK).astype(jnp.float32)
    picked = blocks[:, block_pattern, :]
    output = jnp.einsum("cikp,ikpq->ciq", picked, block_values.astype(jnp.float32))
    return output.reshape(SAMPLES, NODES)


def spatial_back(day_dual, block_values, block_pattern):
    blocks = day_dual.reshape(SAMPLES, BLOCKS, BLOCK).astype(jnp.float32)
    partial_terms = jnp.einsum("ciq,ikpq->ikcp", blocks, block_values.astype(jnp.float32))
    flat = partial_terms.reshape(BLOCKS * LINKS, SAMPLES, BLOCK)
    summed = jax.ops.segment_sum(flat, block_pattern.reshape(-1), num_segments=BLOCKS)
    return jnp.transpose(summed, (1, 0, 2)).reshape(SAMPLES, NODES)


def reference(state, forcing, noise_weight, prev_coupling, next_coupling, block_values, block_pattern):
    rounded = lax.optimization_barrier(state.astype(jnp.bfloat16))
    spatial = lax.map(lambda day: spatial_day(day, block_values, block_pattern), rounded)
    previous = jnp.roll(state, 1, axis=0)
    following = jnp.roll(state, -1, axis=0)
    residual = spatial - prev_coupling * previous - next_coupling * following - forcing
    dual = noise_weight[:, None, :] * residual
    dual_rounded = lax.optimization_barrier(dual.astype(jnp.bfloat16))
    adjoint = lax.map(lambda day: spatial_back(day, block_values, block_pattern), dual_rounded)
    gradient = -(adjoint - prev_coupling * jnp.roll(dual, -1, axis=0) - next_coupling * jnp.roll(dual, 1, axis=0))
    log_density = -0.5 * jnp.sum(residual * dual, axis=(0, 2))
    return gradient, log_density
```

```python
import jax
import jax.numpy as jnp
from jax import lax
from jax.experimental import pallas as pl
from jax.experimental.pallas import tpu as pltpu
from jax.sharding import PartitionSpec as P

MESH = pl.DeviceIdType.MESH
F32 = jnp.float32
BF16 = jnp.bfloat16
LOADS = 8
PIECES = 4


def kernel(
    pat_s, pat_v, pc, nc, state, forcing, weight, values,
    out, dens_out,
    s_v, f_v, w_v, b_v, xr, dr, dual, part, r_first, r_last, w_first, w_last,
    hs_prev, hs_next, hr_prev, hr_next, hw_prev, hw_next, dens, idx_v, idx_s,
    load_sem, b_sem, idx_sem, halo_send, halo_recv, r_send, r_recv, d_send, d_recv,
):
    days, samples, nodes = s_v.shape
    blocks, links, width, _ = b_v.shape
    rows = days * samples
    last = days - 1
    n = lax.axis_size("tm")
    me = lax.axis_index("tm")
    right, left = lax.rem(me + 1, n), lax.rem(me + n - 1, n)

    def cols(i):
        return pl.ds(pl.multiple_of(i * width, width), width)

    loads = [
        pltpu.make_async_copy(state, s_v, load_sem.at[0]),
        pltpu.make_async_copy(forcing, f_v, load_sem.at[1]),
        pltpu.make_async_copy(weight, w_v, load_sem.at[2]),
    ]
    loads[0].start()
    loads[2].start()
    per_load = blocks // LOADS

    def b_load(c):
        span = pl.ds(c * per_load, per_load)
        return pltpu.make_async_copy(values.at[span], b_v.at[span], b_sem.at[c])

    b_load(0).start()
    loads[1].start()
    for c in range(1, LOADS):
        b_load(c).start()

    barrier = pltpu.get_barrier_semaphore()

    @pl.loop(1, n)
    def _(s):
        pl.semaphore_signal(
            barrier, inc=1, device_id={"tm": lax.rem(me + s, n)}, device_id_type=MESH
        )

    pl.semaphore_wait(barrier, n - 1)

    def remote(src, dst, send, recv, target):
        return pltpu.make_async_remote_copy(
            src_ref=src, dst_ref=dst, send_sem=send, recv_sem=recv,
            device_id={"tm": target}, device_id_type=MESH,
        )

    halos = [
        remote(state.at[last], hs_prev, halo_send.at[0], halo_recv.at[0], right),
        remote(state.at[0], hs_next, halo_send.at[1], halo_recv.at[1], left),
    ]
    for copy in halos:
        copy.start()

    lane = lax.broadcasted_iota(jnp.int32, (blocks, blocks), 1)
    sub = lax.broadcasted_iota(jnp.int32, (blocks, blocks), 0)
    none = blocks * links
    idx_v[...] = jnp.zeros_like(idx_v)
    finals = jnp.full((1, blocks), -1, jnp.int32)
    columns = [pat_v[:, k : k + 1] for k in range(links)]
    for k in range(links):
        row = jnp.sum(jnp.where(lane == sub, columns[k], 0), axis=0, keepdims=True)
        found = jnp.full((1, blocks), -1, jnp.int32)
        for q in range(links):
            hit = (columns[q] == row) & (sub < lane)
            found = jnp.maximum(
                found, jnp.max(jnp.where(hit, sub * links + q, -1), axis=0, keepdims=True)
            )
        idx_v[k : k + 1, :blocks] = jnp.where(found < 0, none, found)
        finals = jnp.maximum(
            finals,
            jnp.max(jnp.where(columns[k] == lane, sub * links + k, -1), axis=0, keepdims=True),
        )
    idx_v[links : links + 1, :blocks] = jnp.maximum(finals, 0)
    to_scalar = pltpu.make_async_copy(idx_v, idx_s, idx_sem)
    to_scalar.start()
    part[none] = jnp.zeros((rows, width), F32)

    loads[2].wait()
    w_first[...] = w_v[0:1, :]
    w_last[...] = w_v[last : last + 1, :]
    w_halos = [
        remote(w_last, hw_prev, halo_send.at[2], halo_recv.at[2], right),
        remote(w_first, hw_next, halo_send.at[3], halo_recv.at[3], left),
    ]
    for copy in w_halos:
        copy.start()
    loads[0].wait()

    def round_block(j, _):
        xr[j] = s_v[:, :, cols(j)].reshape(rows, width).astype(BF16)
        return 0

    lax.fori_loop(0, blocks, round_block, 0, unroll=4)
    loads[1].wait()

    def forward(i, total):
        x = jnp.concatenate([xr[pat_s[i, k]] for k in range(links)], axis=1)
        acc = jnp.dot(x, b_v[i].reshape(links * width, width), preferred_element_type=F32)
        acc = acc.reshape(days, samples, width)
        c = cols(i)
        p, q = pc[0:1, c], nc[0:1, c]
        r_first[:, c] = acc[0] - q * s_v[1, :, c] - f_v[0, :, c]
        r_last[:, c] = acc[last] - p * s_v[last - 1, :, c] - f_v[last, :, c]
        for d in range(1, last):
            res = acc[d] - p * s_v[d - 1, :, c] - q * s_v[d + 1, :, c] - f_v[d, :, c]
            du = w_v[d : d + 1, c] * res
            dual[d, :, c] = du
            dr[i, d * samples : (d + 1) * samples, :] = du.astype(BF16)
            total = total + res * du
        return total

    def r_copies(c):
        span = pl.ds(c * (nodes // PIECES), nodes // PIECES)
        return [
            remote(r_last.at[:, span], hr_prev.at[:, span], r_send.at[0, c], r_recv.at[0, c], right),
            remote(r_first.at[:, span], hr_next.at[:, span], r_send.at[1, c], r_recv.at[1, c], left),
        ]

    total = jnp.zeros((samples, width), F32)
    for c in range(LOADS):
        b_load(c).wait()
        total = lax.fori_loop(c * per_load, (c + 1) * per_load, forward, total, unroll=2)
        each = LOADS // PIECES
        if c % each == each - 1:
            for copy in r_copies(c // each):
                copy.start()

    for copy in halos:
        copy.wait_recv()

    def edges(i, total):
        c = cols(i)
        r0 = r_first[:, c] - pc[0:1, c] * hs_prev[:, c]
        r1 = r_last[:, c] - nc[0:1, c] * hs_next[:, c]
        d0 = w_v[0:1, c] * r0
        d1 = w_v[last : last + 1, c] * r1
        dual[0, :, c] = d0
        dual[last, :, c] = d1
        dr[i, 0:samples, :] = d0.astype(BF16)
        dr[i, last * samples :, :] = d1.astype(BF16)
        return total + r0 * d0 + r1 * d1

    total = lax.fori_loop(0, blocks, edges, total, unroll=4)

    sums = -0.5 * jnp.sum(total, axis=1, keepdims=True)
    pick = lax.broadcasted_iota(jnp.int32, (samples, width), 0) == lax.broadcasted_iota(
        jnp.int32, (samples, width), 1
    )
    spread = jnp.sum(jnp.where(pick, sums, 0.0), axis=0, keepdims=True)
    dens[0] = jnp.broadcast_to(spread, dens.shape[1:])

    def d_copy(s):
        return remote(
            dens.at[0], dens.at[s], d_send.at[s], d_recv.at[s], lax.rem(me + s, n)
        )

    @pl.loop(1, n)
    def _(s):
        d_copy(s).start()

    to_scalar.wait()

    def backward(i, _):
        y = lax.dot_general(
            dr[i], b_v[i].reshape(links * width, width),
            (((1,), (1,)), ((), ())), preferred_element_type=F32,
        )
        for k in range(links):
            part[i * links + k] = part[idx_s[k, i]] + y[:, k * width : (k + 1) * width]
        return 0

    lax.fori_loop(0, blocks, backward, 0, unroll=2)

    def gradient(j, _):
        adj = part[idx_s[links, j]].reshape(days, samples, width)
        c = cols(j)
        p, q = pc[0:1, c], nc[0:1, c]
        out[0, :, c] = p * dual[1, :, c] - adj[0]
        out[last, :, c] = q * dual[last - 1, :, c] - adj[last]
        for d in range(1, last):
            out[d, :, c] = p * dual[d + 1, :, c] + q * dual[d - 1, :, c] - adj[d]
        return 0

    lax.fori_loop(0, blocks, gradient, 0, unroll=2)

    for copy in w_halos:
        copy.wait_recv()

    def finish(j, _):
        c = cols(j)
        p, q = pc[0:1, c], nc[0:1, c]
        before = hw_prev[0:1, c] * (hr_prev[:, c] - q * s_v[0, :, c])
        after = hw_next[0:1, c] * (hr_next[:, c] - p * s_v[last, :, c])
        out[0, :, c] = out[0, :, c] + q * before
        out[last, :, c] = out[last, :, c] + p * after
        return 0

    per_piece = blocks // PIECES
    for c in range(PIECES):
        for copy in r_copies(c):
            copy.wait_recv()
        lax.fori_loop(c * per_piece, (c + 1) * per_piece, finish, 0, unroll=4)

    @pl.loop(1, n)
    def _(s):
        d_copy(s).wait()

    def add(s, total):
        return total + dens[s]

    dens_out[...] = lax.fori_loop(1, n, add, dens[0])
    for copy in halos + w_halos:
        copy.wait_send()
    for c in range(PIECES):
        for copy in r_copies(c):
            copy.wait_send()


def shards(state, forcing, noise_weight, prev_coupling, next_coupling, block_values, block_pattern):
    days, samples, nodes = state.shape
    blocks, links, width, _ = block_values.shape
    n = lax.axis_size("tm")
    rows = days * samples
    vmem, sem = pltpu.VMEM, pltpu.SemaphoreType.DMA
    edge = vmem((samples, nodes), F32)
    line = vmem((1, nodes), F32)
    whole = pl.BlockSpec(memory_space=pltpu.VMEM)
    away = pl.BlockSpec(memory_space=pl.ANY)
    gradient, density = pl.pallas_call(
        kernel,
        out_shape=(
            jax.ShapeDtypeStruct((days, samples, nodes), F32),
            jax.ShapeDtypeStruct((8, width), F32),
        ),
        in_specs=[pl.BlockSpec(memory_space=pltpu.SMEM), whole, whole, whole] + [away] * 4,
        out_specs=(whole, whole),
        scratch_shapes=[
            vmem((days, samples, nodes), F32),
            vmem((days, samples, nodes), F32),
            vmem((days, nodes), F32),
            vmem((blocks, links, width, width), BF16),
            vmem((blocks, rows, width), BF16),
            vmem((blocks, rows, width), BF16),
            vmem((days, samples, nodes), F32),
            vmem((blocks * links + 1, rows, width), F32),
            edge, edge, line, line,
            edge, edge, edge, edge, line, line,
            vmem((n, 8, width), F32),
            vmem((8, 128), jnp.int32),
            pltpu.SMEM((8, 128), jnp.int32),
            sem((3,)), sem((LOADS,)), sem,
            sem((4,)), sem((4,)),
            sem((2, PIECES)), sem((2, PIECES)),
            sem((n,)), sem((n,)),
        ],
        compiler_params=pltpu.CompilerParams(
            collective_id=0, has_side_effects=True, vmem_limit_bytes=58 * 2**20
        ),
    )(
        block_pattern, block_pattern,
        prev_coupling.reshape(1, nodes), next_coupling.reshape(1, nodes),
        state, forcing, noise_weight, block_values,
    )
    return gradient, density[0, :samples]


def solution(mesh):
    return jax.shard_map(
        shards,
        mesh=mesh,
        in_specs=(
            P(("grp", "tm"), None, None),
            P(("grp", "tm"), None, None),
            P(("grp", "tm"), None),
            P(),
            P(),
            P(),
            P(),
        ),
        out_specs=(P(("grp", "tm"), None, None), P("grp")),
        check_vma=False,
    )
```

```python
import jax
import jax.numpy as jnp
from jax import lax
from jax.experimental import pallas as pl
from jax.experimental.pallas import tpu as pltpu
from jax.sharding import PartitionSpec as P

MESH = pl.DeviceIdType.MESH
F32 = jnp.float32
BF16 = jnp.bfloat16
LOADS = 8
PIECES = 4


def kernel(
    pat_s, pat_v, pc, nc, state, forcing, weight, values,
    out, dens_out,
    s_v, f_v, w_v, b_v, xr, dr, dual, part, r_first, r_last, w_first, w_last,
    hs_prev, hs_next, hr_prev, hr_next, hw_prev, hw_next, dens, idx_v, idx_s,
    load_sem, b_sem, idx_sem, halo_send, halo_recv, r_send, r_recv, d_send, d_recv,
):
    days, samples, nodes = s_v.shape
    blocks, links, width, _ = b_v.shape
    rows = days * samples
    last = days - 1
    n = lax.axis_size("tm")
    me = lax.axis_index("tm")
    right, left = lax.rem(me + 1, n), lax.rem(me + n - 1, n)

    def cols(i):
        return pl.ds(pl.multiple_of(i * width, width), width)

    loads = [
        pltpu.make_async_copy(state, s_v, load_sem.at[0]),
        pltpu.make_async_copy(forcing, f_v, load_sem.at[1]),
        pltpu.make_async_copy(weight, w_v, load_sem.at[2]),
    ]
    loads[0].start()
    loads[2].start()
    per_load = blocks // LOADS

    def b_load(c):
        span = pl.ds(c * per_load, per_load)
        return pltpu.make_async_copy(values.at[span], b_v.at[span], b_sem.at[c])

    b_load(0).start()
    loads[1].start()
    for c in range(1, LOADS):
        b_load(c).start()

    barrier = pltpu.get_barrier_semaphore()

    @pl.loop(1, n)
    def _(s):
        pl.semaphore_signal(
            barrier, inc=1, device_id={"tm": lax.rem(me + s, n)}, device_id_type=MESH
        )

    pl.semaphore_wait(barrier, n - 1)

    def remote(src, dst, send, recv, target):
        return pltpu.make_async_remote_copy(
            src_ref=src, dst_ref=dst, send_sem=send, recv_sem=recv,
            device_id={"tm": target}, device_id_type=MESH,
        )

    halos = [
        remote(state.at[last], hs_prev, halo_send.at[0], halo_recv.at[0], right),
        remote(state.at[0], hs_next, halo_send.at[1], halo_recv.at[1], left),
    ]
    for copy in halos:
        copy.start()

    lane = lax.broadcasted_iota(jnp.int32, (blocks, blocks), 1)
    sub = lax.broadcasted_iota(jnp.int32, (blocks, blocks), 0)
    none = blocks * links
    idx_v[...] = jnp.zeros_like(idx_v)
    finals = jnp.full((1, blocks), -1, jnp.int32)
    lines = [pat_v[k : k + 1, :] for k in range(links)]
    columns = [
        jnp.sum(jnp.where(lane == sub, line, 0), axis=1, keepdims=True) for line in lines
    ]
    for k in range(links):
        found = jnp.full((1, blocks), -1, jnp.int32)
        for q in range(links):
            hit = (columns[q] == lines[k]) & (sub < lane)
            found = jnp.maximum(
                found, jnp.max(jnp.where(hit, sub * links + q, -1), axis=0, keepdims=True)
            )
        idx_v[k : k + 1, :blocks] = jnp.where(found < 0, none, found)
        finals = jnp.maximum(
            finals,
            jnp.max(jnp.where(columns[k] == lane, sub * links + k, -1), axis=0, keepdims=True),
        )
    idx_v[links : links + 1, :blocks] = jnp.maximum(finals, 0)
    to_scalar = pltpu.make_async_copy(idx_v, idx_s, idx_sem)
    to_scalar.start()
    part[none] = jnp.zeros((rows, width), F32)

    loads[2].wait()
    w_first[...] = w_v[0:1, :]
    w_last[...] = w_v[last : last + 1, :]
    w_halos = [
        remote(w_last, hw_prev, halo_send.at[2], halo_recv.at[2], right),
        remote(w_first, hw_next, halo_send.at[3], halo_recv.at[3], left),
    ]
    for copy in w_halos:
        copy.start()
    loads[0].wait()

    def round_block(j, _):
        xr[j] = s_v[:, :, cols(j)].reshape(rows, width).astype(BF16)
        return 0

    lax.fori_loop(0, blocks, round_block, 0, unroll=4)
    loads[1].wait()

    def forward(i, total):
        x = jnp.concatenate([xr[pat_s[k, i]] for k in range(links)], axis=1)
        acc = jnp.dot(x, b_v[i].reshape(links * width, width), preferred_element_type=F32)
        acc = acc.reshape(days, samples, width)
        c = cols(i)
        p, q = pc[0:1, c], nc[0:1, c]
        r_first[:, c] = acc[0] - q * s_v[1, :, c] - f_v[0, :, c]
        r_last[:, c] = acc[last] - p * s_v[last - 1, :, c] - f_v[last, :, c]
        for d in range(1, last):
            res = acc[d] - p * s_v[d - 1, :, c] - q * s_v[d + 1, :, c] - f_v[d, :, c]
            du = w_v[d : d + 1, c] * res
            dual[d, :, c] = du
            dr[i, d * samples : (d + 1) * samples, :] = du.astype(BF16)
            total = total + res * du
        return total

    def r_copies(c):
        span = pl.ds(c * (nodes // PIECES), nodes // PIECES)
        return [
            remote(r_last.at[:, span], hr_prev.at[:, span], r_send.at[0, c], r_recv.at[0, c], right),
            remote(r_first.at[:, span], hr_next.at[:, span], r_send.at[1, c], r_recv.at[1, c], left),
        ]

    total = jnp.zeros((samples, width), F32)
    for c in range(LOADS):
        b_load(c).wait()
        total = lax.fori_loop(c * per_load, (c + 1) * per_load, forward, total, unroll=2)
        each = LOADS // PIECES
        if c % each == each - 1:
            for copy in r_copies(c // each):
                copy.start()

    for copy in halos:
        copy.wait_recv()

    def edges(i, total):
        c = cols(i)
        r0 = r_first[:, c] - pc[0:1, c] * hs_prev[:, c]
        r1 = r_last[:, c] - nc[0:1, c] * hs_next[:, c]
        d0 = w_v[0:1, c] * r0
        d1 = w_v[last : last + 1, c] * r1
        dual[0, :, c] = d0
        dual[last, :, c] = d1
        dr[i, 0:samples, :] = d0.astype(BF16)
        dr[i, last * samples :, :] = d1.astype(BF16)
        return total + r0 * d0 + r1 * d1

    total = lax.fori_loop(0, blocks, edges, total, unroll=4)

    sums = -0.5 * jnp.sum(total, axis=1, keepdims=True)
    pick = lax.broadcasted_iota(jnp.int32, (samples, width), 0) == lax.broadcasted_iota(
        jnp.int32, (samples, width), 1
    )
    spread = jnp.sum(jnp.where(pick, sums, 0.0), axis=0, keepdims=True)
    dens[0] = jnp.broadcast_to(spread, dens.shape[1:])

    def d_copy(s):
        return remote(
            dens.at[0], dens.at[s], d_send.at[s], d_recv.at[s], lax.rem(me + s, n)
        )

    @pl.loop(1, n)
    def _(s):
        d_copy(s).start()

    to_scalar.wait()

    def backward(i, _):
        y = lax.dot_general(
            dr[i], b_v[i].reshape(links * width, width),
            (((1,), (1,)), ((), ())), preferred_element_type=F32,
        )
        for k in range(links):
            part[i * links + k] = part[idx_s[k, i]] + y[:, k * width : (k + 1) * width]
        return 0

    lax.fori_loop(0, blocks, backward, 0, unroll=2)

    def gradient(j, _):
        adj = part[idx_s[links, j]].reshape(days, samples, width)
        c = cols(j)
        p, q = pc[0:1, c], nc[0:1, c]
        out[0, :, c] = p * dual[1, :, c] - adj[0]
        out[last, :, c] = q * dual[last - 1, :, c] - adj[last]
        for d in range(1, last):
            out[d, :, c] = p * dual[d + 1, :, c] + q * dual[d - 1, :, c] - adj[d]
        return 0

    lax.fori_loop(0, blocks, gradient, 0, unroll=2)

    for copy in w_halos:
        copy.wait_recv()

    def finish(j, _):
        c = cols(j)
        p, q = pc[0:1, c], nc[0:1, c]
        before = hw_prev[0:1, c] * (hr_prev[:, c] - q * s_v[0, :, c])
        after = hw_next[0:1, c] * (hr_next[:, c] - p * s_v[last, :, c])
        out[0, :, c] = out[0, :, c] + q * before
        out[last, :, c] = out[last, :, c] + p * after
        return 0

    per_piece = blocks // PIECES
    for c in range(PIECES):
        for copy in r_copies(c):
            copy.wait_recv()
        lax.fori_loop(c * per_piece, (c + 1) * per_piece, finish, 0, unroll=4)

    @pl.loop(1, n)
    def _(s):
        d_copy(s).wait()

    def add(s, total):
        return total + dens[s]

    dens_out[...] = lax.fori_loop(1, n, add, dens[0])
    for copy in halos + w_halos:
        copy.wait_send()
    for c in range(PIECES):
        for copy in r_copies(c):
            copy.wait_send()


def shards(state, forcing, noise_weight, prev_coupling, next_coupling, block_values, block_pattern):
    days, samples, nodes = state.shape
    blocks, links, width, _ = block_values.shape
    n = lax.axis_size("tm")
    rows = days * samples
    vmem, sem = pltpu.VMEM, pltpu.SemaphoreType.DMA
    edge = vmem((samples, nodes), F32)
    line = vmem((1, nodes), F32)
    whole = pl.BlockSpec(memory_space=pltpu.VMEM)
    away = pl.BlockSpec(memory_space=pl.ANY)
    gradient, density = pl.pallas_call(
        kernel,
        out_shape=(
            pltpu.VMEM((days, samples, nodes), F32),
            pltpu.VMEM((8, width), F32),
        ),
        in_specs=[pl.BlockSpec(memory_space=pltpu.SMEM), whole, whole, whole] + [away] * 4,
        out_specs=(whole, whole),
        scratch_shapes=[
            vmem((days, samples, nodes), F32),
            vmem((days, samples, nodes), F32),
            vmem((days, nodes), F32),
            vmem((blocks, links, width, width), BF16),
            vmem((blocks, rows, width), BF16),
            vmem((blocks, rows, width), BF16),
            vmem((days, samples, nodes), F32),
            vmem((blocks * links + 1, rows, width), F32),
            edge, edge, line, line,
            edge, edge, edge, edge, line, line,
            vmem((n, 8, width), F32),
            vmem((8, 128), jnp.int32),
            pltpu.SMEM((8, 128), jnp.int32),
            sem((3,)), sem((LOADS,)), sem,
            sem((4,)), sem((4,)),
            sem((2, PIECES)), sem((2, PIECES)),
            sem((n,)), sem((n,)),
        ],
        compiler_params=pltpu.CompilerParams(
            collective_id=0, has_side_effects=True, vmem_limit_bytes=58 * 2**20
        ),
    )(
        block_pattern.T, block_pattern.T,
        prev_coupling.reshape(1, nodes), next_coupling.reshape(1, nodes),
        state, forcing, noise_weight, block_values,
    )
    return gradient, density[0, :samples]


def solution(mesh):
    return jax.shard_map(
        shards,
        mesh=mesh,
        in_specs=(
            P(("grp", "tm"), None, None),
            P(("grp", "tm"), None, None),
            P(("grp", "tm"), None),
            P(),
            P(),
            P(),
            P(),
        ),
        out_specs=(P(("grp", "tm"), None, None), P("grp")),
        check_vma=False,
    )
```

```python
import jax
import jax.numpy as jnp
from jax import lax
from jax.experimental import pallas as pl
from jax.experimental.pallas import tpu as pltpu
from jax.sharding import PartitionSpec as P

MESH = pl.DeviceIdType.MESH
F32 = jnp.float32
BF16 = jnp.bfloat16
LOADS = 8
PIECES = 4


def kernel(
    pat_s, pat_v, pc, nc, state, forcing, weight, values,
    out, dens_out,
    s_v, f_v, w_v, b_v, xr, dr, dual, part, r_first, r_last, w_first, w_last,
    hs_prev, hs_next, hr_prev, hr_next, hw_prev, hw_next, dens, idx_v, idx_s,
    load_sem, b_sem, idx_sem, halo_send, halo_recv, r_send, r_recv, d_send, d_recv, gate,
):
    days, samples, nodes = s_v.shape
    blocks, links, width, _ = b_v.shape
    rows = days * samples
    last = days - 1
    n = lax.axis_size("tm")
    me = lax.axis_index("tm")
    right, left = lax.rem(me + 1, n), lax.rem(me + n - 1, n)

    def cols(i):
        return pl.ds(pl.multiple_of(i * width, width), width)

    loads = [
        pltpu.make_async_copy(state, s_v, load_sem.at[0]),
        pltpu.make_async_copy(forcing, f_v, load_sem.at[1]),
        pltpu.make_async_copy(weight, w_v, load_sem.at[2]),
    ]
    loads[0].start()
    loads[2].start()
    per_load = blocks // LOADS

    def b_load(c):
        span = pl.ds(c * per_load, per_load)
        return pltpu.make_async_copy(values.at[span], b_v.at[span], b_sem.at[c])

    b_load(0).start()
    loads[1].start()
    for c in range(1, LOADS):
        b_load(c).start()

    barrier = pltpu.get_barrier_semaphore()

    for peer in (left, right):
        pl.semaphore_signal(barrier, inc=1, device_id={"tm": peer}, device_id_type=MESH)
    pl.semaphore_wait(barrier, 2)

    steps = gate.shape[0]

    def announce(r):
        for far in (1 << r, n - (1 << r)):
            pl.semaphore_signal(
                gate.at[r], inc=1, device_id={"tm": lax.rem(me + far, n)}, device_id_type=MESH
            )

    def learn(r):
        pl.semaphore_wait(gate.at[r], 2)
        if r < steps - 1:
            announce(r + 1)

    def remote(src, dst, send, recv, target):
        return pltpu.make_async_remote_copy(
            src_ref=src, dst_ref=dst, send_sem=send, recv_sem=recv,
            device_id={"tm": target}, device_id_type=MESH,
        )

    halos = [
        remote(state.at[last], hs_prev, halo_send.at[0], halo_recv.at[0], right),
        remote(state.at[0], hs_next, halo_send.at[1], halo_recv.at[1], left),
    ]
    for copy in halos:
        copy.start()
    announce(0)

    lane = lax.broadcasted_iota(jnp.int32, (blocks, blocks), 1)
    sub = lax.broadcasted_iota(jnp.int32, (blocks, blocks), 0)
    none = blocks * links
    idx_v[...] = jnp.zeros_like(idx_v)
    finals = jnp.full((1, blocks), -1, jnp.int32)
    lines = [pat_v[k : k + 1, :] for k in range(links)]
    columns = [
        jnp.sum(jnp.where(lane == sub, line, 0), axis=1, keepdims=True) for line in lines
    ]
    for k in range(links):
        found = jnp.full((1, blocks), -1, jnp.int32)
        for q in range(links):
            hit = (columns[q] == lines[k]) & (sub < lane)
            found = jnp.maximum(
                found, jnp.max(jnp.where(hit, sub * links + q, -1), axis=0, keepdims=True)
            )
        idx_v[k : k + 1, :blocks] = jnp.where(found < 0, none, found)
        finals = jnp.maximum(
            finals,
            jnp.max(jnp.where(columns[k] == lane, sub * links + k, -1), axis=0, keepdims=True),
        )
    idx_v[links : links + 1, :blocks] = jnp.maximum(finals, 0)
    to_scalar = pltpu.make_async_copy(idx_v, idx_s, idx_sem)
    to_scalar.start()
    part[none] = jnp.zeros((rows, width), F32)

    loads[2].wait()
    w_first[...] = w_v[0:1, :]
    w_last[...] = w_v[last : last + 1, :]
    w_halos = [
        remote(w_last, hw_prev, halo_send.at[2], halo_recv.at[2], right),
        remote(w_first, hw_next, halo_send.at[3], halo_recv.at[3], left),
    ]
    for copy in w_halos:
        copy.start()
    loads[0].wait()

    def round_block(j, _):
        xr[j] = s_v[:, :, cols(j)].reshape(rows, width).astype(BF16)
        return 0

    lax.fori_loop(0, blocks, round_block, 0, unroll=4)
    loads[1].wait()

    def forward(i, total):
        x = jnp.concatenate([xr[pat_s[k, i]] for k in range(links)], axis=1)
        acc = jnp.dot(x, b_v[i].reshape(links * width, width), preferred_element_type=F32)
        acc = acc.reshape(days, samples, width)
        c = cols(i)
        p, q = pc[0:1, c], nc[0:1, c]
        r_first[:, c] = acc[0] - q * s_v[1, :, c] - f_v[0, :, c]
        r_last[:, c] = acc[last] - p * s_v[last - 1, :, c] - f_v[last, :, c]
        for d in range(1, last):
            res = acc[d] - p * s_v[d - 1, :, c] - q * s_v[d + 1, :, c] - f_v[d, :, c]
            du = w_v[d : d + 1, c] * res
            dual[d, :, c] = du
            dr[i, d * samples : (d + 1) * samples, :] = du.astype(BF16)
            total = total + res * du
        return total

    def r_copies(c):
        span = pl.ds(c * (nodes // PIECES), nodes // PIECES)
        return [
            remote(r_last.at[:, span], hr_prev.at[:, span], r_send.at[0, c], r_recv.at[0, c], right),
            remote(r_first.at[:, span], hr_next.at[:, span], r_send.at[1, c], r_recv.at[1, c], left),
        ]

    total = jnp.zeros((samples, width), F32)
    for c in range(LOADS):
        b_load(c).wait()
        if c < steps:
            learn(c)
        total = lax.fori_loop(c * per_load, (c + 1) * per_load, forward, total, unroll=2)
        each = LOADS // PIECES
        if c % each == each - 1:
            for copy in r_copies(c // each):
                copy.start()

    for copy in halos:
        copy.wait_recv()

    def edges(i, total):
        c = cols(i)
        r0 = r_first[:, c] - pc[0:1, c] * hs_prev[:, c]
        r1 = r_last[:, c] - nc[0:1, c] * hs_next[:, c]
        d0 = w_v[0:1, c] * r0
        d1 = w_v[last : last + 1, c] * r1
        dual[0, :, c] = d0
        dual[last, :, c] = d1
        dr[i, 0:samples, :] = d0.astype(BF16)
        dr[i, last * samples :, :] = d1.astype(BF16)
        return total + r0 * d0 + r1 * d1

    total = lax.fori_loop(0, blocks, edges, total, unroll=4)

    sums = -0.5 * jnp.sum(total, axis=1, keepdims=True)
    pick = lax.broadcasted_iota(jnp.int32, (samples, width), 0) == lax.broadcasted_iota(
        jnp.int32, (samples, width), 1
    )
    spread = jnp.sum(jnp.where(pick, sums, 0.0), axis=0, keepdims=True)
    dens[0] = jnp.broadcast_to(spread, dens.shape[1:])

    def d_copy(s):
        return remote(
            dens.at[0], dens.at[s], d_send.at[s], d_recv.at[s], lax.rem(me + s, n)
        )

    @pl.loop(1, n)
    def _(s):
        d_copy(s).start()

    to_scalar.wait()

    def backward(i, _):
        y = lax.dot_general(
            dr[i], b_v[i].reshape(links * width, width),
            (((1,), (1,)), ((), ())), preferred_element_type=F32,
        )
        for k in range(links):
            part[i * links + k] = part[idx_s[k, i]] + y[:, k * width : (k + 1) * width]
        return 0

    lax.fori_loop(0, blocks, backward, 0, unroll=2)

    def gradient(j, _):
        adj = part[idx_s[links, j]].reshape(days, samples, width)
        c = cols(j)
        p, q = pc[0:1, c], nc[0:1, c]
        out[0, :, c] = p * dual[1, :, c] - adj[0]
        out[last, :, c] = q * dual[last - 1, :, c] - adj[last]
        for d in range(1, last):
            out[d, :, c] = p * dual[d + 1, :, c] + q * dual[d - 1, :, c] - adj[d]
        return 0

    lax.fori_loop(0, blocks, gradient, 0, unroll=2)

    for copy in w_halos:
        copy.wait_recv()

    def finish(j, _):
        c = cols(j)
        p, q = pc[0:1, c], nc[0:1, c]
        before = hw_prev[0:1, c] * (hr_prev[:, c] - q * s_v[0, :, c])
        after = hw_next[0:1, c] * (hr_next[:, c] - p * s_v[last, :, c])
        out[0, :, c] = out[0, :, c] + q * before
        out[last, :, c] = out[last, :, c] + p * after
        return 0

    per_piece = blocks // PIECES
    for c in range(PIECES):
        for copy in r_copies(c):
            copy.wait_recv()
        lax.fori_loop(c * per_piece, (c + 1) * per_piece, finish, 0, unroll=4)

    @pl.loop(1, n)
    def _(s):
        d_copy(s).wait()

    def add(s, total):
        return total + dens[s]

    dens_out[...] = lax.fori_loop(1, n, add, dens[0])
    for copy in halos + w_halos:
        copy.wait_send()
    for c in range(PIECES):
        for copy in r_copies(c):
            copy.wait_send()


def shards(state, forcing, noise_weight, prev_coupling, next_coupling, block_values, block_pattern):
    days, samples, nodes = state.shape
    blocks, links, width, _ = block_values.shape
    n = lax.axis_size("tm")
    rows = days * samples
    vmem, sem = pltpu.VMEM, pltpu.SemaphoreType.DMA
    edge = vmem((samples, nodes), F32)
    line = vmem((1, nodes), F32)
    whole = pl.BlockSpec(memory_space=pltpu.VMEM)
    away = pl.BlockSpec(memory_space=pl.ANY)
    gradient, density = pl.pallas_call(
        kernel,
        out_shape=(
            pltpu.VMEM((days, samples, nodes), F32),
            pltpu.VMEM((8, width), F32),
        ),
        in_specs=[pl.BlockSpec(memory_space=pltpu.SMEM), whole, whole, whole] + [away] * 4,
        out_specs=(whole, whole),
        scratch_shapes=[
            vmem((days, samples, nodes), F32),
            vmem((days, samples, nodes), F32),
            vmem((days, nodes), F32),
            vmem((blocks, links, width, width), BF16),
            vmem((blocks, rows, width), BF16),
            vmem((blocks, rows, width), BF16),
            vmem((days, samples, nodes), F32),
            vmem((blocks * links + 1, rows, width), F32),
            edge, edge, line, line,
            edge, edge, edge, edge, line, line,
            vmem((n, 8, width), F32),
            vmem((8, 128), jnp.int32),
            pltpu.SMEM((8, 128), jnp.int32),
            sem((3,)), sem((LOADS,)), sem,
            sem((4,)), sem((4,)),
            sem((2, PIECES)), sem((2, PIECES)),
            sem((n,)), sem((n,)),
            pltpu.SemaphoreType.REGULAR((max(1, (n // 2 - 1).bit_length()),)),
        ],
        compiler_params=pltpu.CompilerParams(
            collective_id=0, has_side_effects=True, vmem_limit_bytes=58 * 2**20
        ),
    )(
        block_pattern.T, block_pattern.T,
        prev_coupling.reshape(1, nodes), next_coupling.reshape(1, nodes),
        state, forcing, noise_weight, block_values,
    )
    return gradient, density[0, :samples]


def solution(mesh):
    return jax.shard_map(
        shards,
        mesh=mesh,
        in_specs=(
            P(("grp", "tm"), None, None),
            P(("grp", "tm"), None, None),
            P(("grp", "tm"), None),
            P(),
            P(),
            P(),
            P(),
        ),
        out_specs=(P(("grp", "tm"), None, None), P("grp")),
        check_vma=False,
    )
```

```python
import jax
import jax.numpy as jnp
from jax import lax
from jax.experimental import pallas as pl
from jax.experimental.pallas import tpu as pltpu
from jax.sharding import PartitionSpec as P

MESH = pl.DeviceIdType.MESH
F32 = jnp.float32
BF16 = jnp.bfloat16
LOADS = 8
PIECES = 4


def kernel(
    pat_s, pat_v, pc, nc, state, forcing, weight, values,
    out, dens_out,
    s_v, f_v, w_v, b_v, xr, dr, dual, part, r_first, r_last, w_first, w_last,
    hs_prev, hs_next, hr_prev, hr_next, hw_prev, hw_next, dens, idx_v, idx_s,
    load_sem, b_sem, idx_sem, halo_send, halo_recv, r_send, r_recv, d_send, d_recv, gate,
):
    days, samples, nodes = s_v.shape
    blocks, links, width, _ = b_v.shape
    rows = days * samples
    last = days - 1
    n = lax.axis_size("tm")
    me = lax.axis_index("tm")
    right, left = lax.rem(me + 1, n), lax.rem(me + n - 1, n)

    def cols(i):
        return pl.ds(pl.multiple_of(i * width, width), width)

    loads = [
        pltpu.make_async_copy(state, s_v, load_sem.at[0]),
        pltpu.make_async_copy(forcing, f_v, load_sem.at[1]),
        pltpu.make_async_copy(weight, w_v, load_sem.at[2]),
    ]
    loads[0].start()
    loads[2].start()
    per_load = blocks // LOADS

    def b_load(c):
        span = pl.ds(c * per_load, per_load)
        return pltpu.make_async_copy(values.at[span], b_v.at[span], b_sem.at[c])

    b_load(0).start()
    loads[1].start()
    for c in range(1, LOADS):
        b_load(c).start()

    barrier = pltpu.get_barrier_semaphore()

    for peer in (left, right):
        pl.semaphore_signal(barrier, inc=1, device_id={"tm": peer}, device_id_type=MESH)
    pl.semaphore_wait(barrier, 2)

    steps = gate.shape[0]

    def announce(r):
        for far in (1 << r, n - (1 << r)):
            pl.semaphore_signal(
                gate.at[r], inc=1, device_id={"tm": lax.rem(me + far, n)}, device_id_type=MESH
            )

    def learn(r):
        pl.semaphore_wait(gate.at[r], 2)
        if r < steps - 1:
            announce(r + 1)

    def remote(src, dst, send, recv, target):
        return pltpu.make_async_remote_copy(
            src_ref=src, dst_ref=dst, send_sem=send, recv_sem=recv,
            device_id={"tm": target}, device_id_type=MESH,
        )

    halos = [
        remote(state.at[last], hs_prev, halo_send.at[0], halo_recv.at[0], right),
        remote(state.at[0], hs_next, halo_send.at[1], halo_recv.at[1], left),
    ]
    for copy in halos:
        copy.start()
    announce(0)

    lane = lax.broadcasted_iota(jnp.int32, (blocks, blocks), 1)
    sub = lax.broadcasted_iota(jnp.int32, (blocks, blocks), 0)
    none = blocks * links
    idx_v[...] = jnp.zeros_like(idx_v)
    finals = jnp.full((1, blocks), -1, jnp.int32)
    lines = [pat_v[k : k + 1, :] for k in range(links)]
    columns = [
        jnp.sum(jnp.where(lane == sub, line, 0), axis=1, keepdims=True) for line in lines
    ]
    for k in range(links):
        found = jnp.full((1, blocks), -1, jnp.int32)
        for q in range(links):
            hit = (columns[q] == lines[k]) & (sub < lane)
            found = jnp.maximum(
                found, jnp.max(jnp.where(hit, sub * links + q, -1), axis=0, keepdims=True)
            )
        idx_v[k : k + 1, :blocks] = jnp.where(found < 0, none, found)
        finals = jnp.maximum(
            finals,
            jnp.max(jnp.where(columns[k] == lane, sub * links + k, -1), axis=0, keepdims=True),
        )
    idx_v[links : links + 1, :blocks] = jnp.maximum(finals, 0)
    to_scalar = pltpu.make_async_copy(idx_v, idx_s, idx_sem)
    to_scalar.start()
    part[none] = jnp.zeros((rows, width), F32)

    loads[2].wait()
    w_first[...] = w_v[0:1, :]
    w_last[...] = w_v[last : last + 1, :]
    w_halos = [
        remote(w_last, hw_prev, halo_send.at[2], halo_recv.at[2], right),
        remote(w_first, hw_next, halo_send.at[3], halo_recv.at[3], left),
    ]
    for copy in w_halos:
        copy.start()
    loads[0].wait()

    def round_block(j, _):
        xr[j] = s_v[:, :, cols(j)].reshape(rows, width).astype(BF16)
        return 0

    lax.fori_loop(0, blocks, round_block, 0, unroll=4)
    loads[1].wait()

    def forward(i, total):
        x = jnp.concatenate([xr[pat_s[k, i]] for k in range(links)], axis=1)
        acc = jnp.dot(x, b_v[i].reshape(links * width, width), preferred_element_type=F32)
        acc = acc.reshape(days, samples, width)
        c = cols(i)
        p, q = pc[0:1, c], nc[0:1, c]
        r_first[:, c] = acc[0] - q * s_v[1, :, c] - f_v[0, :, c]
        r_last[:, c] = acc[last] - p * s_v[last - 1, :, c] - f_v[last, :, c]
        for d in range(1, last):
            res = acc[d] - p * s_v[d - 1, :, c] - q * s_v[d + 1, :, c] - f_v[d, :, c]
            du = w_v[d : d + 1, c] * res
            dual[d, :, c] = du
            dr[i, d * samples : (d + 1) * samples, :] = du.astype(BF16)
            total = total + res * du
        return total

    def r_copies(c):
        span = pl.ds(c * (nodes // PIECES), nodes // PIECES)
        return [
            remote(r_last.at[:, span], hr_prev.at[:, span], r_send.at[0, c], r_recv.at[0, c], right),
            remote(r_first.at[:, span], hr_next.at[:, span], r_send.at[1, c], r_recv.at[1, c], left),
        ]

    total = jnp.zeros((samples, width), F32)
    for c in range(LOADS):
        b_load(c).wait()
        if c < steps:
            learn(c)
        total = lax.fori_loop(c * per_load, (c + 1) * per_load, forward, total, unroll=4)
        each = LOADS // PIECES
        if c % each == each - 1:
            for copy in r_copies(c // each):
                copy.start()

    for copy in halos:
        copy.wait_recv()

    def edges(i, total):
        c = cols(i)
        r0 = r_first[:, c] - pc[0:1, c] * hs_prev[:, c]
        r1 = r_last[:, c] - nc[0:1, c] * hs_next[:, c]
        d0 = w_v[0:1, c] * r0
        d1 = w_v[last : last + 1, c] * r1
        dual[0, :, c] = d0
        dual[last, :, c] = d1
        dr[i, 0:samples, :] = d0.astype(BF16)
        dr[i, last * samples :, :] = d1.astype(BF16)
        return total + r0 * d0 + r1 * d1

    total = lax.fori_loop(0, blocks, edges, total, unroll=4)

    sums = -0.5 * jnp.sum(total, axis=1, keepdims=True)
    pick = lax.broadcasted_iota(jnp.int32, (samples, width), 0) == lax.broadcasted_iota(
        jnp.int32, (samples, width), 1
    )
    spread = jnp.sum(jnp.where(pick, sums, 0.0), axis=0, keepdims=True)
    dens[0] = jnp.broadcast_to(spread, dens.shape[1:])

    def d_copy(s):
        return remote(
            dens.at[0], dens.at[s], d_send.at[s], d_recv.at[s], lax.rem(me + s, n)
        )

    @pl.loop(1, n)
    def _(s):
        d_copy(s).start()

    to_scalar.wait()

    def backward(i, _):
        y = lax.dot_general(
            dr[i], b_v[i].reshape(links * width, width),
            (((1,), (1,)), ((), ())), preferred_element_type=F32,
        )
        for k in range(links):
            part[i * links + k] = part[idx_s[k, i]] + y[:, k * width : (k + 1) * width]
        return 0

    lax.fori_loop(0, blocks, backward, 0, unroll=4)

    def gradient(j, _):
        adj = part[idx_s[links, j]].reshape(days, samples, width)
        c = cols(j)
        p, q = pc[0:1, c], nc[0:1, c]
        out[0, :, c] = p * dual[1, :, c] - adj[0]
        out[last, :, c] = q * dual[last - 1, :, c] - adj[last]
        for d in range(1, last):
            out[d, :, c] = p * dual[d + 1, :, c] + q * dual[d - 1, :, c] - adj[d]
        return 0

    lax.fori_loop(0, blocks, gradient, 0, unroll=4)

    for copy in w_halos:
        copy.wait_recv()

    def finish(j, _):
        c = cols(j)
        p, q = pc[0:1, c], nc[0:1, c]
        before = hw_prev[0:1, c] * (hr_prev[:, c] - q * s_v[0, :, c])
        after = hw_next[0:1, c] * (hr_next[:, c] - p * s_v[last, :, c])
        out[0, :, c] = out[0, :, c] + q * before
        out[last, :, c] = out[last, :, c] + p * after
        return 0

    per_piece = blocks // PIECES
    for c in range(PIECES):
        for copy in r_copies(c):
            copy.wait_recv()
        lax.fori_loop(c * per_piece, (c + 1) * per_piece, finish, 0, unroll=4)

    @pl.loop(1, n)
    def _(s):
        d_copy(s).wait()

    def add(s, total):
        return total + dens[s]

    dens_out[...] = lax.fori_loop(1, n, add, dens[0])
    for copy in halos + w_halos:
        copy.wait_send()
    for c in range(PIECES):
        for copy in r_copies(c):
            copy.wait_send()


def shards(state, forcing, noise_weight, prev_coupling, next_coupling, block_values, block_pattern):
    days, samples, nodes = state.shape
    blocks, links, width, _ = block_values.shape
    n = lax.axis_size("tm")
    rows = days * samples
    vmem, sem = pltpu.VMEM, pltpu.SemaphoreType.DMA
    edge = vmem((samples, nodes), F32)
    line = vmem((1, nodes), F32)
    whole = pl.BlockSpec(memory_space=pltpu.VMEM)
    away = pl.BlockSpec(memory_space=pl.ANY)
    gradient, density = pl.pallas_call(
        kernel,
        out_shape=(
            pltpu.VMEM((days, samples, nodes), F32),
            pltpu.VMEM((8, width), F32),
        ),
        in_specs=[pl.BlockSpec(memory_space=pltpu.SMEM), whole, whole, whole] + [away] * 4,
        out_specs=(whole, whole),
        scratch_shapes=[
            vmem((days, samples, nodes), F32),
            vmem((days, samples, nodes), F32),
            vmem((days, nodes), F32),
            vmem((blocks, links, width, width), BF16),
            vmem((blocks, rows, width), BF16),
            vmem((blocks, rows, width), BF16),
            vmem((days, samples, nodes), F32),
            vmem((blocks * links + 1, rows, width), F32),
            edge, edge, line, line,
            edge, edge, edge, edge, line, line,
            vmem((n, 8, width), F32),
            vmem((8, 128), jnp.int32),
            pltpu.SMEM((8, 128), jnp.int32),
            sem((3,)), sem((LOADS,)), sem,
            sem((4,)), sem((4,)),
            sem((2, PIECES)), sem((2, PIECES)),
            sem((n,)), sem((n,)),
            pltpu.SemaphoreType.REGULAR((max(1, (n // 2 - 1).bit_length()),)),
        ],
        compiler_params=pltpu.CompilerParams(
            collective_id=0, has_side_effects=True, vmem_limit_bytes=58 * 2**20
        ),
    )(
        block_pattern.T, block_pattern.T,
        prev_coupling.reshape(1, nodes), next_coupling.reshape(1, nodes),
        state, forcing, noise_weight, block_values,
    )
    return gradient, density[0, :samples]


def solution(mesh):
    return jax.shard_map(
        shards,
        mesh=mesh,
        in_specs=(
            P(("grp", "tm"), None, None),
            P(("grp", "tm"), None, None),
            P(("grp", "tm"), None),
            P(),
            P(),
            P(),
            P(),
        ),
        out_specs=(P(("grp", "tm"), None, None), P("grp")),
        check_vma=False,
    )
```
